32 devices in a mesh: groups: 2 (over y), expert: 4 (over z), cuts: 4 (over x, core).
Axes of the slice: x: 2, y: 2, z: 4, core: 2. Of those that a mesh axis runs over, the one named last changes fastest.
Arguments:
- queries: bfloat16 [256, 6144], P(('groups', 'expert'), 'cuts'), parts along dimension 0, may hold values from -108 to 108
- key_cache: bfloat16 [256, 96, 1024], P(('groups', 'expert'), None, 'cuts'), parts along dimension 0, may hold values from -4.5 to 4.5
- value_cache: bfloat16 [256, 96, 1024], P(('groups', 'expert'), None, 'cuts'), parts along dimension 0, may hold values from -6 to 6
- lengths: int32 [256], P(('groups', 'expert')), parts along dimension 0, may hold values from 1 to 96, as said below
- residual: bfloat16 [256, 6144], P(('groups', 'expert'), 'cuts'), parts along dimension 0, may hold values from -6 to 6
- routes: int32 [256, 4], P(('groups', 'expert')), parts along dimension 0, may hold values from 0 to 15, all different within a row; in each aligned block of 32 rows (0 to 31, 32 to 63, ...) at most 8 rows name the same one
- route_weight: float32 [256, 4], P(('groups', 'expert')), parts along dimension 0, may hold values from 0.2 to 1
- gate_weight: bfloat16 [4, 6144, 4096], P('expert', None, 'cuts'), may hold values from -0.078125 to 0.078125
- up_weight: bfloat16 [4, 6144, 4096], P('expert', None, 'cuts'), may hold values from -0.078125 to 0.078125
- down_weight: bfloat16 [4, 4096, 6144], P('expert', 'cuts'), may hold values from -0.0625 to 0.0625
Outputs:
- layer_out: bfloat16 [256, 6144], P(('groups', 'expert'), 'cuts'), parts along dimension 0
The draws below stay inside these ranges and needn't reach their ends.
There are 2 independent parts, one for each index of `groups`. The reference program is written for one: setup_inputs(seed, part) draws one part's arguments, and reference() takes and returns one part's arrays. A program takes and returns all parts, laid end to end along the dimension named above; an argument that names none is the same for every part. Nothing has to cross between parts.
Inputs may be any that keep to these rules, and one draw needn't show every extreme that they name: `lengths`: the first row of each device's block of 32 rows has length 96. `routes`: each row names 4 different experts; within each device's block of 32 rows no expert is named by more than 8 rows.
All inputs are finite; a program needn't handle non-finite values.
Results may differ from the reference program's by a relative error of at most 0.007.
Values may be sent and summed in bfloat16 or wider, within the bound.
A program may use at most 128 MiB of HBM per device.

```python
import math
import jax
import jax.numpy as jnp
import numpy as np
from jax import lax

D = 6144
HEADS = 48
KV_HEADS = 8
HEAD = 128
MODEL_EXPERTS = 16
TOPK = 4
EXPERTS = 2
FF = 8192
ROW_DEV = 32
CTX = 96
SPLIT = 2
FF_DEV = 1024
CAP = 8
ROWS = 128
N_CUTS = 4


def shared_keys(key):
    drawn = jax.random.normal(jax.random.fold_in(key, 11), (ROWS, CTX, KV_HEADS * HEAD), jnp.float32)
    drawn = jnp.clip(drawn, -4.5, 4.5)
    position = jnp.arange(CTX)
    return jnp.where((position == CTX - 2)[None, :, None], 0.99 * drawn[:, CTX - 1:CTX, :], drawn)


def draw_key_cache(key, part):
    shared = shared_keys(key)
    return shared.astype(jnp.bfloat16)


def draw_queries(key, part):
    key = jax.random.fold_in(key, 5)
    result = jnp.clip(jax.random.normal(key, (ROWS, HEADS * HEAD), jnp.float32), -5.0, 5.0)
    return result.astype(jnp.bfloat16)


def draw_lengths(key, part):
    key = jax.random.fold_in(key, 7)
    drawn = jax.random.randint(key, (ROWS,), 1, CTX + 1, dtype=jnp.int32)
    return jnp.where(jnp.arange(ROWS) % ROW_DEV == 0, CTX, drawn).astype(jnp.int32)


def block_scale(own_key, extent, cuts, least, high):
    gain, own = 1.0, jax.random.fold_in(own_key, 6)
    for dim, blocks in cuts:
        draws = jnp.exp(jax.random.uniform(jax.random.fold_in(own, dim), (blocks,), jnp.float32, least / len(cuts), high / len(cuts)))
        gain = gain * jnp.repeat(draws, extent[dim] // blocks).reshape([-1 if axis == dim else 1 for axis in range(len(extent))])
    return gain


def routed_block(stream_key, own, number, rows, count, top, bound, lean):
    order = jax.random.permutation(stream_key, count)
    packed, common = portions_of(count, rows * top, bound, lean, True), portions_of(count, rows * top, bound, lean, False)
    places = jnp.arange(count)

    def named(sizes, offset_by):
        used = int((sizes > 0).sum())
        fixed = max(1, used // 4)
        passed = fixed + (places - fixed + offset_by * (used - fixed)) % max(1, count - fixed)
        return jnp.zeros((count,), jnp.int32).at[order[jnp.where(places < fixed, places, passed)]].set(jnp.asarray(sizes, jnp.int32))

    sizes = jnp.where(number % 4 == 0, named(packed, number // 4), named(common, number - number // 4 - 1))
    mixed = jax.random.permutation(jax.random.fold_in(own, 3), count)
    source_of, taker = mixed[0:count // 2 * 2:2], mixed[1:count // 2 * 2:2]
    margin = jnp.minimum(sizes[source_of] - 1, bound - sizes[taker]) // 2
    margin = jnp.where((source_of == order[0]) | (taker == order[0]) | (sizes[taker] == 0), 0, jnp.maximum(margin, 0))
    passed = jax.random.randint(jax.random.fold_in(own, 4), (count // 2,), 0, 1 << 20) % (margin + 1)
    sizes = sizes.at[source_of].add(-passed).at[taker].add(passed)
    items = jnp.searchsorted(jnp.cumsum(sizes), jnp.arange(rows * top), side="right").astype(jnp.int32)
    listing = items.reshape(top, rows).T
    listing = listing[jax.random.permutation(jax.random.fold_in(own, 1), rows)]
    offset_by = jax.random.randint(jax.random.fold_in(own, 2), (rows, 1), 0, top)
    return jnp.take_along_axis(listing, (jnp.arange(top)[None, :] + offset_by) % top, axis=1)


def portions_of(amount, total, bound, skew, full):
    loads = [(1 << 20) // math.isqrt(grade ** skew) + 1 for grade in range(1, amount + 1)]
    largest = bound if full else min(bound, max(-(-total // amount), total * loads[0] // sum(loads)))
    least = 1 if total - largest >= amount - 1 else 0
    holding, surplus = [largest] + [least] * (amount - 1), total - largest - least * (amount - 1)
    while surplus > 0:
        candidates = [i for i in range(1, amount) if holding[i] < largest] or [i for i in range(1, amount) if holding[i] < bound]
        mass, budget = sum([loads[i] for i in candidates]), surplus
        for i in candidates:
            extra = min(bound - holding[i], max(1, budget * loads[i] // mass), surplus)
            holding[i] = holding[i] + extra
            surplus = surplus - extra
    return np.array(holding)


def scatter_about(own_key, dims, width, most, cuts=(), kind=jnp.bfloat16):
    gain = block_scale(own_key, dims, cuts, -0.22, 0.18) if cuts else 1.0
    values = jax.random.normal(own_key, dims, jnp.float32) * width * gain
    return jnp.minimum(jnp.maximum(values, -most), most).astype(kind)


def setup_inputs(seed: int = 0, part: int = 0) -> dict:
    streams_of = jax.random.split(jax.random.key(seed), 11)
    part_splits = jax.random.split(jax.random.fold_in(streams_of[10], part), 11)
    queries = draw_queries(jax.random.fold_in(jax.random.fold_in(streams_of[10], part), 71), part)
    key_cache = draw_key_cache(jax.random.fold_in(jax.random.fold_in(streams_of[10], part), 71), part)
    value_cache = scatter_about(part_splits[2], (ROWS, CTX, KV_HEADS * HEAD), 1.0, 6.0, ((0, 4), (2, 4)))
    lengths = draw_lengths(jax.random.fold_in(jax.random.fold_in(streams_of[10], part), 71), part)
    residual = scatter_about(part_splits[4], (ROWS, D), 1.0, 6.0, ((0, 4), (1, 4)))
    routes_keys = jax.random.split(jax.random.fold_in(part_splits[5], 1), ROWS // ROW_DEV)
    routes_turns = jax.random.permutation(jax.random.fold_in(part_splits[5], 3), ROWS // ROW_DEV)
    routes = jax.vmap(lambda own, number: routed_block(jax.random.fold_in(part_splits[5], 2), own, number, ROW_DEV, MODEL_EXPERTS, TOPK, CAP, 2))(routes_keys, routes_turns).reshape((ROWS, TOPK))
    route_weight = jnp.clip(0.2 + 0.8 * jax.random.uniform(part_splits[6], (ROWS, TOPK), jnp.float32) ** block_scale(part_splits[6], (ROWS, TOPK), ((0, 4),), -0.2, 0.2), 0.2, 1.0)
    gate_weight = scatter_about(streams_of[7], (EXPERTS * SPLIT, D, FF_DEV * N_CUTS), D ** -0.5, 0.078125, ((0, 4), (2, 4)))
    up_weight = scatter_about(streams_of[8], (EXPERTS * SPLIT, D, FF_DEV * N_CUTS), D ** -0.5, 0.078125, ((0, 4), (2, 4)))
    down_weight = scatter_about(streams_of[9], (EXPERTS * SPLIT, FF_DEV * N_CUTS, D), FF ** -0.5, 0.0625, ((0, 4), (1, 4)))
    return dict(queries=queries, key_cache=key_cache, value_cache=value_cache, lengths=lengths, residual=residual, routes=routes, route_weight=route_weight, gate_weight=gate_weight, up_weight=up_weight, down_weight=down_weight)


def reference(queries, key_cache, value_cache, lengths, residual, routes, route_weight, gate_weight, up_weight, down_weight):
    group_size = HEADS // KV_HEADS
    query_heads = queries.reshape(ROWS, KV_HEADS, group_size, HEAD).astype(jnp.float32)
    key_heads = key_cache.reshape(ROWS, CTX, KV_HEADS, HEAD).astype(jnp.float32)
    scores = jnp.einsum('rkgj,rtkj->rkgt', query_heads, key_heads) / math.sqrt(HEAD)
    visible = jnp.arange(CTX, dtype=jnp.int32)[None, None, None, :] < lengths[:, None, None, None]
    scores = jnp.where(visible, scores, -jnp.inf)
    highest = lax.optimization_barrier(jnp.max(scores, axis=-1, keepdims=True))
    scaled = jnp.exp(scores - highest)
    probabilities = (scaled / lax.optimization_barrier(jnp.sum(scaled, axis=-1, keepdims=True))).astype(jnp.bfloat16)
    value_heads = value_cache.reshape(ROWS, CTX, KV_HEADS, HEAD).astype(jnp.float32)
    attended = jnp.einsum('rkgt,rtkj->rkgj', probabilities.astype(jnp.float32), value_heads).reshape(ROWS, D)
    hidden = residual.astype(jnp.float32) + attended
    inputs = hidden.astype(jnp.bfloat16)
    expert_ids = jnp.arange(EXPERTS, dtype=jnp.int32)
    onehot = (routes[:, :, None] == expert_ids[None, None, :]).astype(jnp.float32)
    coefficients = lax.optimization_barrier(jnp.sum(onehot * route_weight[:, :, None], axis=1))

    def one_slice(running, pieces):
        gate_part, up_part, down_part, slice_index = pieces
        gate_act = jnp.dot(inputs, gate_part, preferred_element_type=jnp.float32)
        up_act = jnp.dot(inputs, up_part, preferred_element_type=jnp.float32)
        activated = (jax.nn.silu(gate_act) * up_act).astype(jnp.bfloat16)
        produced = jnp.dot(activated, down_part, preferred_element_type=jnp.float32)
        column = lax.optimization_barrier(jnp.sum(coefficients * (expert_ids == slice_index // SPLIT).astype(jnp.float32)[None, :], axis=1))
        return (running + column[:, None] * produced, None)
    slice_ids = jnp.arange(EXPERTS * SPLIT, dtype=jnp.int32)
    combined, _ = lax.scan(one_slice, jnp.zeros((ROWS, D), jnp.float32), (gate_weight, up_weight, down_weight, slice_ids))
    return (hidden + combined).astype(jnp.bfloat16)
```

```python
import functools
import math

import jax
import jax.numpy as jnp
from jax import lax
from jax.experimental import pallas as pl
from jax.experimental.pallas import tpu as pltpu
from jax.sharding import PartitionSpec as P

HEADS = 48
KV_HEADS = 8
HEAD = 128
MODEL_EXPERTS = 16
TOPK = 4
EXPERTS = 2
SLOTS = 8
MESH = pl.DeviceIdType.MESH


def each(low, high, body):
    if high - low <= 8:
        for i in range(low, high):
            body(i)
    else:

        def step(i, carry):
            body(i)
            return carry

        lax.fori_loop(low, high, step, 0)


def cut_order(c, cuts):
    if cuts == 4:
        beside = c + 1 - 2 * lax.rem(c, 2)
        return [c, beside, lax.rem(c + 2, 4), lax.rem(beside + 2, 4)]
    return [lax.rem(c + i, cuts) for i in range(cuts)]


def kernel(
    devices,
    cuts,
    cap,
    lengths,
    routes,
    route_weight,
    queries,
    keys,
    values,
    residual,
    gate,
    up,
    down,
    out,
    q_buf,
    k_buf,
    v_buf,
    res_buf,
    q_rows,
    att_rows,
    hidden,
    wg,
    wu,
    wd,
    outgoing,
    arrived,
    stacked,
    gate_act,
    up_act,
    act,
    cut_send,
    cut_recv,
    own,
    back_send,
    back_recv,
    in_sem,
    wg_sem,
    wu_sem,
    wd_sem,
    row_send,
    row_recv,
    share_send,
    share_recv,
    sum_send,
    sum_recv,
    ret_send,
    ret_recv,
):
    b = lax.axis_index("expert")
    c = lax.axis_index("cuts")
    order = cut_order(c, cuts)
    row_count, width = q_buf.shape
    context = k_buf.shape[1]
    kv_local = k_buf.shape[2] // HEAD
    group = HEADS // KV_HEADS
    stride = kv_local * SLOTS
    splits = devices // EXPERTS
    half = width // 2
    ff = wg.shape[2]

    barrier = pltpu.get_barrier_semaphore()

    def greet(i):
        pl.semaphore_signal(
            barrier, inc=1, device_id={"expert": lax.rem(b + i, devices)}, device_id_type=MESH
        )

    each(1, devices, greet)
    for peer in order[1:]:
        pl.semaphore_signal(barrier, inc=1, device_id={"cuts": peer}, device_id_type=MESH)

    loads = [
        pltpu.make_async_copy(queries, q_buf, in_sem.at[0]),
        pltpu.make_async_copy(keys, k_buf, in_sem.at[1]),
        pltpu.make_async_copy(values, v_buf, in_sem.at[2]),
        pltpu.make_async_copy(residual, res_buf, in_sem.at[3]),
    ]
    gate_loads, up_loads, down_loads = [], [], []
    for i in range(cuts):
        rows = pl.ds(pl.multiple_of(order[i] * width, width), width)
        gate_loads.append(pltpu.make_async_copy(gate.at[0, rows, :], wg.at[i], wg_sem.at[i]))
        up_loads.append(pltpu.make_async_copy(up.at[0, rows, :], wu.at[i], wu_sem.at[i]))
    for i in range(cuts):
        columns = pl.ds(pl.multiple_of(order[cuts - 1 - i] * width, width), width)
        down_loads.append(pltpu.make_async_copy(down.at[0, :, columns], wd.at[i], wd_sem.at[i]))
    for load in loads:
        load.start()
    for g, u in zip(gate_loads, up_loads):
        g.start()
        u.start()
    for d in down_loads:
        d.start()

    slot = lax.broadcasted_iota(jnp.int32, (EXPERTS * cap, row_count), 0)
    expert_of = slot // cap
    routed = jnp.zeros((EXPERTS * cap, row_count), jnp.float32)
    share = jnp.zeros((EXPERTS * cap, row_count), jnp.float32)
    for k in range(TOPK):
        named = routes[k : k + 1, :] == expert_of
        routed = routed + jnp.where(named, 1.0, 0.0)
        share = share + jnp.where(named, route_weight[k : k + 1, :], 0.0)
    before = jnp.where(
        lax.broadcasted_iota(jnp.int32, (row_count, row_count), 0)
        < lax.broadcasted_iota(jnp.int32, (row_count, row_count), 1),
        1.0,
        0.0,
    )
    earlier = jnp.dot(
        routed.astype(jnp.bfloat16), before.astype(jnp.bfloat16), preferred_element_type=jnp.float32
    )
    place = (slot - expert_of * cap).astype(jnp.float32)
    chosen = jnp.where(earlier == place, routed, 0.0)
    weighted = chosen * share

    q_rows[...] = jnp.zeros_like(q_rows)
    loads[0].wait()
    for kv in range(kv_local):
        for g in range(group):
            head = kv * group + g
            q_rows[pl.ds(kv * SLOTS + g, row_count, stride=stride), :] = q_buf[
                :, head * HEAD : (head + 1) * HEAD
            ].astype(jnp.float32)
    loads[1].wait()
    loads[2].wait()
    key_head = lax.broadcasted_iota(jnp.int32, (stride, HEAD), 0) // SLOTS
    position = lax.broadcasted_iota(jnp.int32, (stride, context), 1)
    block = 8

    def attend(blk, carry):
        for i in range(block):
            r = blk * block + i
            start = pl.multiple_of(r * stride, stride)
            q = q_rows[pl.ds(start, stride), :]
            q = jnp.concatenate(
                [jnp.where(key_head == kv, q, 0.0) for kv in range(kv_local)], axis=1
            ).astype(jnp.bfloat16)
            scores = lax.dot_general(
                q, k_buf[r], (((1,), (1,)), ((), ())), preferred_element_type=jnp.float32
            ) / math.sqrt(HEAD)
            scores = jnp.where(position < lengths[r], scores, -jnp.inf)
            scaled = jnp.exp(scores - jnp.max(scores, axis=-1, keepdims=True))
            prob = (scaled / jnp.sum(scaled, axis=-1, keepdims=True)).astype(jnp.bfloat16)
            att = jnp.dot(prob, v_buf[r], preferred_element_type=jnp.float32)
            for kv in range(kv_local):
                att_rows[pl.ds(start + kv * SLOTS, SLOTS), :] = att[
                    kv * SLOTS : (kv + 1) * SLOTS, kv * HEAD : (kv + 1) * HEAD
                ]
        return carry

    lax.fori_loop(0, row_count // block, attend, 0)
    loads[3].wait()
    for kv in range(kv_local):
        for g in range(group):
            columns = slice((kv * group + g) * HEAD, (kv * group + g + 1) * HEAD)
            hidden[:, columns] = (
                res_buf[:, columns].astype(jnp.float32)
                + att_rows[pl.ds(kv * SLOTS + g, row_count, stride=stride), :]
            )

    picked = jnp.dot(
        chosen.astype(jnp.bfloat16),
        hidden[...].astype(jnp.bfloat16),
        preferred_element_type=jnp.float32,
    )
    for e in range(EXPERTS):
        rows = picked[e * cap : (e + 1) * cap]
        outgoing[e] = jnp.concatenate([rows[:, :half], rows[:, half:]], axis=0).astype(jnp.bfloat16)
    arrived[c, b] = outgoing[b // splits]

    pl.semaphore_wait(barrier, devices - 1 + cuts - 1)

    def row_copy(to):
        return pltpu.make_async_remote_copy(
            src_ref=outgoing.at[to // splits],
            dst_ref=arrived.at[c, b],
            send_sem=row_send.at[to],
            recv_sem=row_recv.at[b],
            device_id={"expert": to},
            device_id_type=MESH,
        )

    each(1, devices, lambda i: row_copy(lax.rem(b + i, devices)).start())

    def forward(a):
        for peer in order[:0:-1]:
            pltpu.make_async_remote_copy(
                src_ref=arrived.at[c, a],
                dst_ref=arrived.at[c, a],
                send_sem=share_send.at[peer],
                recv_sem=share_recv.at[c],
                device_id={"cuts": peer},
                device_id_type=MESH,
            ).start()

    forward(b)

    def take(i):
        a = lax.rem(b + devices - i, devices)
        pltpu.make_async_remote_copy(
            src_ref=arrived.at[c, a],
            dst_ref=arrived.at[c, a],
            send_sem=row_send.at[a],
            recv_sem=row_recv.at[a],
            device_id={"expert": a},
            device_id_type=MESH,
        ).wait_recv()
        forward(a)

    each(1, devices, take)

    def whole_share(peer):
        return pltpu.make_async_remote_copy(
            src_ref=arrived.at[peer],
            dst_ref=arrived.at[peer],
            send_sem=share_send.at[peer],
            recv_sem=share_recv.at[peer],
            device_id={"cuts": peer},
            device_id_type=MESH,
        )

    tile = 512 if ff % 512 == 0 else ff
    for i in range(cuts):
        if i:
            whole_share(order[i]).wait_recv()

        def pack(pair, i=i):
            first = arrived[order[i], 2 * pair].astype(jnp.float32)
            second = arrived[order[i], 2 * pair + 1].astype(jnp.float32)
            rows = pl.ds(pair * 2 * cap, 2 * cap)
            stacked[rows, :half] = jnp.concatenate([first[:cap], second[:cap]], axis=0).astype(
                jnp.bfloat16
            )
            stacked[rows, half:] = jnp.concatenate([first[cap:], second[cap:]], axis=0).astype(
                jnp.bfloat16
            )

        each(0, devices // 2, pack)
        gate_loads[i].wait()
        up_loads[i].wait()

        def project(n, carry, i=i):
            columns = pl.ds(pl.multiple_of(n * tile, tile), tile)
            x = stacked[...]
            for weight, total in ((wg, gate_act), (wu, up_act)):
                part = jnp.dot(x, weight[i, :, columns], preferred_element_type=jnp.float32)
                total[:, columns] = part if i == 0 else total[:, columns] + part
            return carry

        lax.fori_loop(0, ff // tile, project, 0)

    gated = gate_act[...]
    act[...] = (gated / (1.0 + jnp.exp(-gated)) * up_act[...]).astype(jnp.bfloat16)

    def sum_copy(j):
        peer = order[cuts - 1 - j]
        return pltpu.make_async_remote_copy(
            src_ref=cut_send.at[j],
            dst_ref=cut_recv.at[c],
            send_sem=sum_send.at[j],
            recv_sem=sum_recv.at[c],
            device_id={"cuts": peer},
            device_id_type=MESH,
        )

    out_tile = half if half % 128 == 0 else width
    for j in range(cuts):
        down_loads[j].wait()

        def expand(n, carry, j=j):
            columns = pl.ds(pl.multiple_of(n * out_tile, out_tile), out_tile)
            part = jnp.dot(act[...], wd[j, :, columns], preferred_element_type=jnp.float32)
            if j < cuts - 1:
                cut_send[j, :, columns] = part.astype(jnp.bfloat16)
            else:
                own[:, columns] = part
            return carry

        lax.fori_loop(0, width // out_tile, expand, 0)
        if j < cuts - 1:
            sum_copy(j).start()

    for peer in order[1:]:
        pltpu.make_async_remote_copy(
            src_ref=cut_recv.at[peer],
            dst_ref=cut_recv.at[peer],
            send_sem=sum_send.at[0],
            recv_sem=sum_recv.at[peer],
            device_id={"cuts": peer},
            device_id_type=MESH,
        ).wait_recv()

    def total(pair):
        rows = pl.ds(pair * 2 * cap, 2 * cap)
        value = own[rows, :]
        for peer in order[1:]:
            value = value + cut_recv[peer, rows, :].astype(jnp.float32)
        for k in range(2):
            mine = value[k * cap : (k + 1) * cap]
            back_send[2 * pair + k] = jnp.concatenate(
                [mine[:, :half], mine[:, half:]], axis=0
            ).astype(jnp.bfloat16)

    each(0, devices // 2, total)

    def back_copy(to):
        return pltpu.make_async_remote_copy(
            src_ref=back_send.at[to],
            dst_ref=back_recv.at[b],
            send_sem=ret_send.at[to],
            recv_sem=ret_recv.at[b],
            device_id={"expert": to},
            device_id_type=MESH,
        )

    each(1, devices, lambda i: back_copy(lax.rem(b + i, devices)).start())
    back_recv[b] = back_send[b]

    each(1, devices, lambda i: row_copy(lax.rem(b + i, devices)).wait_send())
    for peer in order[1:]:
        whole_share(peer).wait_send()
    for j in range(cuts - 1):
        sum_copy(j).wait_send()

    def returned(i):
        a = lax.rem(b + devices - i, devices)
        pltpu.make_async_remote_copy(
            src_ref=back_recv.at[a],
            dst_ref=back_recv.at[a],
            send_sem=ret_send.at[a],
            recv_sem=ret_recv.at[a],
            device_id={"expert": a},
            device_id_type=MESH,
        ).wait_recv()

    each(1, devices, returned)
    sums = []
    for e in range(EXPERTS):
        value = back_recv[e * splits].astype(jnp.float32)
        for s in range(1, splits):
            value = value + back_recv[e * splits + s].astype(jnp.float32)
        sums.append(value)
    for h in range(2):
        columns = slice(h * half, (h + 1) * half)
        stack = jnp.concatenate([value[h * cap : (h + 1) * cap] for value in sums], axis=0)
        combined = lax.dot_general(
            weighted,
            stack,
            (((0,), (0,)), ((), ())),
            preferred_element_type=jnp.float32,
            precision=lax.Precision.HIGHEST,
        )
        out[:, columns] = (hidden[:, columns] + combined).astype(jnp.bfloat16)
    each(1, devices, lambda i: back_copy(lax.rem(b + i, devices)).wait_send())


def on_device(
    devices,
    cuts,
    queries,
    key_cache,
    value_cache,
    lengths,
    residual,
    routes,
    route_weight,
    gate_weight,
    up_weight,
    down_weight,
):
    row_count, width = queries.shape
    cap = (row_count * TOPK + MODEL_EXPERTS - 1) // MODEL_EXPERTS
    ff = gate_weight.shape[2]
    kv_width = key_cache.shape[2]
    stride = kv_width // HEAD * SLOTS
    items = devices * cap
    bf16, f32 = jnp.bfloat16, jnp.float32
    dma = pltpu.SemaphoreType.DMA
    vmem = pl.BlockSpec(memory_space=pltpu.VMEM)
    anywhere = pl.BlockSpec(memory_space=pl.ANY)
    return pl.pallas_call(
        functools.partial(kernel, devices, cuts, cap),
        out_shape=jax.ShapeDtypeStruct((row_count, width), bf16),
        in_specs=[pl.BlockSpec(memory_space=pltpu.SMEM), vmem, vmem] + [anywhere] * 7,
        out_specs=vmem,
        scratch_shapes=[
            pltpu.VMEM((row_count, width), bf16),
            pltpu.VMEM(key_cache.shape, bf16),
            pltpu.VMEM(value_cache.shape, bf16),
            pltpu.VMEM((row_count, width), bf16),
            pltpu.VMEM((row_count * stride, HEAD), f32),
            pltpu.VMEM((row_count * stride, HEAD), f32),
            pltpu.VMEM((row_count, width), f32),
            pltpu.VMEM((cuts, width, ff), bf16),
            pltpu.VMEM((cuts, width, ff), bf16),
            pltpu.VMEM((cuts, ff, width), bf16),
            pltpu.VMEM((EXPERTS, 2 * cap, width // 2), bf16),
            pltpu.VMEM((cuts, devices, 2 * cap, width // 2), bf16),
            pltpu.VMEM((items, width), bf16),
            pltpu.VMEM((items, ff), f32),
            pltpu.VMEM((items, ff), f32),
            pltpu.VMEM((items, ff), bf16),
            pltpu.VMEM((cuts - 1, items, width), bf16),
            pltpu.VMEM((cuts, items, width), bf16),
            pltpu.VMEM((items, width), f32),
            pltpu.VMEM((devices, 2 * cap, width // 2), bf16),
            pltpu.VMEM((devices, 2 * cap, width // 2), bf16),
            dma((4,)),
            dma((cuts,)),
            dma((cuts,)),
            dma((cuts,)),
            dma((devices,)),
            dma((devices,)),
            dma((cuts,)),
            dma((cuts,)),
            dma((cuts - 1,)),
            dma((cuts,)),
            dma((devices,)),
            dma((devices,)),
        ],
        compiler_params=pltpu.CompilerParams(
            collective_id=0, has_side_effects=True, vmem_limit_bytes=60 * 1024 * 1024
        ),
    )(
        lengths,
        routes.T,
        route_weight.T,
        queries,
        key_cache,
        value_cache,
        residual,
        gate_weight,
        up_weight,
        down_weight,
    )


def solution(mesh):
    return jax.shard_map(
        functools.partial(on_device, mesh.shape["expert"], mesh.shape["cuts"]),
        mesh=mesh,
        in_specs=(
            P(("groups", "expert"), "cuts"),
            P(("groups", "expert"), None, "cuts"),
            P(("groups", "expert"), None, "cuts"),
            P(("groups", "expert")),
            P(("groups", "expert"), "cuts"),
            P(("groups", "expert"), None),
            P(("groups", "expert"), None),
            P("expert", None, "cuts"),
            P("expert", None, "cuts"),
            P("expert", "cuts", None),
        ),
        out_specs=P(("groups", "expert"), "cuts"),
        check_vma=False,
    )
```

```python
import functools
import math

import jax
import jax.numpy as jnp
from jax import lax
from jax.experimental import pallas as pl
from jax.experimental.pallas import tpu as pltpu
from jax.sharding import PartitionSpec as P

HEADS = 48
KV_HEADS = 8
HEAD = 128
MODEL_EXPERTS = 16
TOPK = 4
EXPERTS = 2
SLOTS = 8
MESH = pl.DeviceIdType.MESH


def each(low, high, body):
    if high - low <= 8:
        for i in range(low, high):
            body(i)
    else:

        def step(i, carry):
            body(i)
            return carry

        lax.fori_loop(low, high, step, 0)


def cut_order(c, cuts):
    if cuts == 4:
        beside = c + 1 - 2 * lax.rem(c, 2)
        return [c, beside, lax.rem(c + 2, 4), lax.rem(beside + 2, 4)]
    return [lax.rem(c + i, cuts) for i in range(cuts)]


def kernel(
    devices,
    cuts,
    cap,
    lengths,
    routes,
    route_weight,
    queries,
    keys,
    values,
    residual,
    gate,
    up,
    down,
    out,
    q_buf,
    k_buf,
    v_buf,
    res_buf,
    q_rows,
    att_rows,
    hidden,
    wg,
    wu,
    wd,
    outgoing,
    arrived,
    stacked,
    gate_act,
    up_act,
    act,
    cut_send,
    cut_recv,
    own,
    back_send,
    back_recv,
    in_sem,
    wg_sem,
    wu_sem,
    wd_sem,
    row_send,
    row_recv,
    share_send,
    share_recv,
    sum_send,
    sum_recv,
    ret_send,
    ret_recv,
):
    b = lax.axis_index("expert")
    c = lax.axis_index("cuts")
    order = cut_order(c, cuts)
    row_count, width = q_buf.shape
    context = k_buf.shape[1]
    kv_local = k_buf.shape[2] // HEAD
    group = HEADS // KV_HEADS
    stride = kv_local * SLOTS
    splits = devices // EXPERTS
    half = width // 2
    ff = wg.shape[2]

    barrier = pltpu.get_barrier_semaphore()

    def greet(i):
        pl.semaphore_signal(
            barrier, inc=1, device_id={"expert": lax.rem(b + i, devices)}, device_id_type=MESH
        )

    each(1, devices, greet)
    for peer in order[1:]:
        pl.semaphore_signal(barrier, inc=1, device_id={"cuts": peer}, device_id_type=MESH)

    loads = [
        pltpu.make_async_copy(queries, q_buf, in_sem.at[0]),
        pltpu.make_async_copy(keys, k_buf, in_sem.at[1]),
        pltpu.make_async_copy(values, v_buf, in_sem.at[2]),
        pltpu.make_async_copy(residual, res_buf, in_sem.at[3]),
    ]
    gate_loads, up_loads, down_loads = [], [], []
    for i in range(cuts):
        rows = pl.ds(pl.multiple_of(order[i] * width, width), width)
        gate_loads.append(pltpu.make_async_copy(gate.at[0, rows, :], wg.at[i], wg_sem.at[i]))
        up_loads.append(pltpu.make_async_copy(up.at[0, rows, :], wu.at[i], wu_sem.at[i]))
    for i in range(cuts):
        columns = pl.ds(pl.multiple_of(order[cuts - 1 - i] * width, width), width)
        down_loads.append(pltpu.make_async_copy(down.at[0, :, columns], wd.at[i], wd_sem.at[i]))
    for load in loads:
        load.start()

    slot = lax.broadcasted_iota(jnp.int32, (EXPERTS * cap, row_count), 0)
    expert_of = slot // cap
    routed = jnp.zeros((EXPERTS * cap, row_count), jnp.float32)
    share = jnp.zeros((EXPERTS * cap, row_count), jnp.float32)
    for k in range(TOPK):
        named = routes[k : k + 1, :] == expert_of
        routed = routed + jnp.where(named, 1.0, 0.0)
        share = share + jnp.where(named, route_weight[k : k + 1, :], 0.0)
    before = jnp.where(
        lax.broadcasted_iota(jnp.int32, (row_count, row_count), 0)
        < lax.broadcasted_iota(jnp.int32, (row_count, row_count), 1),
        1.0,
        0.0,
    )
    earlier = jnp.dot(
        routed.astype(jnp.bfloat16), before.astype(jnp.bfloat16), preferred_element_type=jnp.float32
    )
    place = (slot - expert_of * cap).astype(jnp.float32)
    chosen = jnp.where(earlier == place, routed, 0.0)
    weighted = chosen * share

    q_rows[...] = jnp.zeros_like(q_rows)
    loads[0].wait()
    for kv in range(kv_local):
        for g in range(group):
            head = kv * group + g
            q_rows[pl.ds(kv * SLOTS + g, row_count, stride=stride), :] = q_buf[
                :, head * HEAD : (head + 1) * HEAD
            ].astype(jnp.float32)
    loads[1].wait()
    loads[2].wait()
    for g, u in zip(gate_loads, up_loads):
        g.start()
        u.start()
    for d in down_loads:
        d.start()
    key_head = lax.broadcasted_iota(jnp.int32, (stride, HEAD), 0) // SLOTS
    position = lax.broadcasted_iota(jnp.int32, (stride, context), 1)
    block = min(16, row_count)

    def attend(blk, carry):
        rows = [blk * block + i for i in range(block)]
        starts = [pl.multiple_of(r * stride, stride) for r in rows]
        scores, probs = [], []
        for r, start in zip(rows, starts):
            q = q_rows[pl.ds(start, stride), :]
            q = jnp.concatenate(
                [jnp.where(key_head == kv, q, 0.0) for kv in range(kv_local)], axis=1
            ).astype(jnp.bfloat16)
            scores.append(
                lax.dot_general(
                    q, k_buf[r], (((1,), (1,)), ((), ())), preferred_element_type=jnp.float32
                )
            )
        scores = [
            jnp.where(position < lengths[r], score / math.sqrt(HEAD), -jnp.inf)
            for r, score in zip(rows, scores)
        ]
        highest = [jnp.max(score, axis=-1, keepdims=True) for score in scores]
        scaled = [jnp.exp(score - high) for score, high in zip(scores, highest)]
        sums = [jnp.sum(value, axis=-1, keepdims=True) for value in scaled]
        probs = [(value / part).astype(jnp.bfloat16) for value, part in zip(scaled, sums)]
        atts = [
            jnp.dot(prob, v_buf[r], preferred_element_type=jnp.float32)
            for r, prob in zip(rows, probs)
        ]
        for start, att in zip(starts, atts):
            for kv in range(kv_local):
                att_rows[pl.ds(start + kv * SLOTS, SLOTS), :] = att[
                    kv * SLOTS : (kv + 1) * SLOTS, kv * HEAD : (kv + 1) * HEAD
                ]
        return carry

    lax.fori_loop(0, row_count // block, attend, 0)
    loads[3].wait()
    for kv in range(kv_local):
        for g in range(group):
            columns = slice((kv * group + g) * HEAD, (kv * group + g + 1) * HEAD)
            hidden[:, columns] = (
                res_buf[:, columns].astype(jnp.float32)
                + att_rows[pl.ds(kv * SLOTS + g, row_count, stride=stride), :]
            )

    picked = jnp.dot(
        chosen.astype(jnp.bfloat16),
        hidden[...].astype(jnp.bfloat16),
        preferred_element_type=jnp.float32,
    )
    for e in range(EXPERTS):
        rows = picked[e * cap : (e + 1) * cap]
        outgoing[e] = jnp.concatenate([rows[:, :half], rows[:, half:]], axis=0).astype(jnp.bfloat16)
    arrived[c, b] = outgoing[b // splits]

    pl.semaphore_wait(barrier, devices - 1 + cuts - 1)

    def row_copy(to):
        return pltpu.make_async_remote_copy(
            src_ref=outgoing.at[to // splits],
            dst_ref=arrived.at[c, b],
            send_sem=row_send.at[to],
            recv_sem=row_recv.at[b],
            device_id={"expert": to},
            device_id_type=MESH,
        )

    each(1, devices, lambda i: row_copy(lax.rem(b + i, devices)).start())

    def forward(a):
        for peer in order[:0:-1]:
            pltpu.make_async_remote_copy(
                src_ref=arrived.at[c, a],
                dst_ref=arrived.at[c, a],
                send_sem=share_send.at[peer],
                recv_sem=share_recv.at[c],
                device_id={"cuts": peer},
                device_id_type=MESH,
            ).start()

    forward(b)

    def take(i):
        a = lax.rem(b + devices - i, devices)
        pltpu.make_async_remote_copy(
            src_ref=arrived.at[c, a],
            dst_ref=arrived.at[c, a],
            send_sem=row_send.at[a],
            recv_sem=row_recv.at[a],
            device_id={"expert": a},
            device_id_type=MESH,
        ).wait_recv()
        forward(a)

    each(1, devices, take)

    def whole_share(peer):
        return pltpu.make_async_remote_copy(
            src_ref=arrived.at[peer],
            dst_ref=arrived.at[peer],
            send_sem=share_send.at[peer],
            recv_sem=share_recv.at[peer],
            device_id={"cuts": peer},
            device_id_type=MESH,
        )

    tile = 512 if ff % 512 == 0 else ff
    for i in range(cuts):
        if i:
            whole_share(order[i]).wait_recv()

        def pack(pair, i=i):
            first = arrived[order[i], 2 * pair].astype(jnp.float32)
            second = arrived[order[i], 2 * pair + 1].astype(jnp.float32)
            rows = pl.ds(pair * 2 * cap, 2 * cap)
            stacked[rows, :half] = jnp.concatenate([first[:cap], second[:cap]], axis=0).astype(
                jnp.bfloat16
            )
            stacked[rows, half:] = jnp.concatenate([first[cap:], second[cap:]], axis=0).astype(
                jnp.bfloat16
            )

        each(0, devices // 2, pack)
        gate_loads[i].wait()
        up_loads[i].wait()

        def project(n, carry, i=i):
            columns = pl.ds(pl.multiple_of(n * tile, tile), tile)
            x = stacked[...]
            for weight, total in ((wg, gate_act), (wu, up_act)):
                part = jnp.dot(x, weight[i, :, columns], preferred_element_type=jnp.float32)
                total[:, columns] = part if i == 0 else total[:, columns] + part
            return carry

        lax.fori_loop(0, ff // tile, project, 0)

    gated = gate_act[...]
    act[...] = (gated / (1.0 + jnp.exp(-gated)) * up_act[...]).astype(jnp.bfloat16)

    def sum_copy(j):
        peer = order[cuts - 1 - j]
        return pltpu.make_async_remote_copy(
            src_ref=cut_send.at[j],
            dst_ref=cut_recv.at[c],
            send_sem=sum_send.at[j],
            recv_sem=sum_recv.at[c],
            device_id={"cuts": peer},
            device_id_type=MESH,
        )

    out_tile = half if half % 128 == 0 else width
    for j in range(cuts):
        down_loads[j].wait()

        def expand(n, carry, j=j):
            columns = pl.ds(pl.multiple_of(n * out_tile, out_tile), out_tile)
            part = jnp.dot(act[...], wd[j, :, columns], preferred_element_type=jnp.float32)
            if j < cuts - 1:
                cut_send[j, :, columns] = part.astype(jnp.bfloat16)
            else:
                own[:, columns] = part
            return carry

        lax.fori_loop(0, width // out_tile, expand, 0)
        if j < cuts - 1:
            sum_copy(j).start()

    for peer in order[1:]:
        pltpu.make_async_remote_copy(
            src_ref=cut_recv.at[peer],
            dst_ref=cut_recv.at[peer],
            send_sem=sum_send.at[0],
            recv_sem=sum_recv.at[peer],
            device_id={"cuts": peer},
            device_id_type=MESH,
        ).wait_recv()

    def total(pair):
        rows = pl.ds(pair * 2 * cap, 2 * cap)
        value = own[rows, :]
        for peer in order[1:]:
            value = value + cut_recv[peer, rows, :].astype(jnp.float32)
        for k in range(2):
            mine = value[k * cap : (k + 1) * cap]
            back_send[2 * pair + k] = jnp.concatenate(
                [mine[:, :half], mine[:, half:]], axis=0
            ).astype(jnp.bfloat16)

    each(0, devices // 2, total)

    def back_copy(to):
        return pltpu.make_async_remote_copy(
            src_ref=back_send.at[to],
            dst_ref=back_recv.at[b],
            send_sem=ret_send.at[to],
            recv_sem=ret_recv.at[b],
            device_id={"expert": to},
            device_id_type=MESH,
        )

    each(1, devices, lambda i: back_copy(lax.rem(b + i, devices)).start())
    back_recv[b] = back_send[b]

    each(1, devices, lambda i: row_copy(lax.rem(b + i, devices)).wait_send())
    for peer in order[1:]:
        whole_share(peer).wait_send()
    for j in range(cuts - 1):
        sum_copy(j).wait_send()

    def returned(i):
        a = lax.rem(b + devices - i, devices)
        pltpu.make_async_remote_copy(
            src_ref=back_recv.at[a],
            dst_ref=back_recv.at[a],
            send_sem=ret_send.at[a],
            recv_sem=ret_recv.at[a],
            device_id={"expert": a},
            device_id_type=MESH,
        ).wait_recv()

    each(1, devices, returned)
    sums = []
    for e in range(EXPERTS):
        value = back_recv[e * splits].astype(jnp.float32)
        for s in range(1, splits):
            value = value + back_recv[e * splits + s].astype(jnp.float32)
        sums.append(value)
    for h in range(2):
        columns = slice(h * half, (h + 1) * half)
        stack = jnp.concatenate([value[h * cap : (h + 1) * cap] for value in sums], axis=0)
        combined = lax.dot_general(
            weighted,
            stack,
            (((0,), (0,)), ((), ())),
            preferred_element_type=jnp.float32,
            precision=lax.Precision.HIGHEST,
        )
        out[:, columns] = (hidden[:, columns] + combined).astype(jnp.bfloat16)
    each(1, devices, lambda i: back_copy(lax.rem(b + i, devices)).wait_send())


def on_device(
    devices,
    cuts,
    queries,
    key_cache,
    value_cache,
    lengths,
    residual,
    routes,
    route_weight,
    gate_weight,
    up_weight,
    down_weight,
):
    row_count, width = queries.shape
    cap = (row_count * TOPK + MODEL_EXPERTS - 1) // MODEL_EXPERTS
    ff = gate_weight.shape[2]
    kv_width = key_cache.shape[2]
    stride = kv_width // HEAD * SLOTS
    items = devices * cap
    bf16, f32 = jnp.bfloat16, jnp.float32
    dma = pltpu.SemaphoreType.DMA
    vmem = pl.BlockSpec(memory_space=pltpu.VMEM)
    anywhere = pl.BlockSpec(memory_space=pl.ANY)
    return pl.pallas_call(
        functools.partial(kernel, devices, cuts, cap),
        out_shape=jax.ShapeDtypeStruct((row_count, width), bf16),
        in_specs=[pl.BlockSpec(memory_space=pltpu.SMEM), vmem, vmem] + [anywhere] * 7,
        out_specs=vmem,
        scratch_shapes=[
            pltpu.VMEM((row_count, width), bf16),
            pltpu.VMEM(key_cache.shape, bf16),
            pltpu.VMEM(value_cache.shape, bf16),
            pltpu.VMEM((row_count, width), bf16),
            pltpu.VMEM((row_count * stride, HEAD), f32),
            pltpu.VMEM((row_count * stride, HEAD), f32),
            pltpu.VMEM((row_count, width), f32),
            pltpu.VMEM((cuts, width, ff), bf16),
            pltpu.VMEM((cuts, width, ff), bf16),
            pltpu.VMEM((cuts, ff, width), bf16),
            pltpu.VMEM((EXPERTS, 2 * cap, width // 2), bf16),
            pltpu.VMEM((cuts, devices, 2 * cap, width // 2), bf16),
            pltpu.VMEM((items, width), bf16),
            pltpu.VMEM((items, ff), f32),
            pltpu.VMEM((items, ff), f32),
            pltpu.VMEM((items, ff), bf16),
            pltpu.VMEM((cuts - 1, items, width), bf16),
            pltpu.VMEM((cuts, items, width), bf16),
            pltpu.VMEM((items, width), f32),
            pltpu.VMEM((devices, 2 * cap, width // 2), bf16),
            pltpu.VMEM((devices, 2 * cap, width // 2), bf16),
            dma((4,)),
            dma((cuts,)),
            dma((cuts,)),
            dma((cuts,)),
            dma((devices,)),
            dma((devices,)),
            dma((cuts,)),
            dma((cuts,)),
            dma((cuts - 1,)),
            dma((cuts,)),
            dma((devices,)),
            dma((devices,)),
        ],
        compiler_params=pltpu.CompilerParams(
            collective_id=0, has_side_effects=True, vmem_limit_bytes=60 * 1024 * 1024
        ),
    )(
        lengths,
        routes.T,
        route_weight.T,
        queries,
        key_cache,
        value_cache,
        residual,
        gate_weight,
        up_weight,
        down_weight,
    )


def solution(mesh):
    return jax.shard_map(
        functools.partial(on_device, mesh.shape["expert"], mesh.shape["cuts"]),
        mesh=mesh,
        in_specs=(
            P(("groups", "expert"), "cuts"),
            P(("groups", "expert"), None, "cuts"),
            P(("groups", "expert"), None, "cuts"),
            P(("groups", "expert")),
            P(("groups", "expert"), "cuts"),
            P(("groups", "expert"), None),
            P(("groups", "expert"), None),
            P("expert", None, "cuts"),
            P("expert", None, "cuts"),
            P("expert", "cuts", None),
        ),
        out_specs=P(("groups", "expert"), "cuts"),
        check_vma=False,
    )
```

```python
import functools
import math

import jax
import jax.numpy as jnp
from jax import lax
from jax.experimental import pallas as pl
from jax.experimental.pallas import tpu as pltpu
from jax.sharding import PartitionSpec as P

HEADS = 48
KV_HEADS = 8
HEAD = 128
MODEL_EXPERTS = 16
TOPK = 4
EXPERTS = 2
SLOTS = 8
MESH = pl.DeviceIdType.MESH


def each(low, high, body):
    if high - low <= 8:
        for i in range(low, high):
            body(i)
    else:

        def step(i, carry):
            body(i)
            return carry

        lax.fori_loop(low, high, step, 0)


def cut_order(c, cuts):
    if cuts == 4:
        beside = c + 1 - 2 * lax.rem(c, 2)
        return [c, beside, lax.rem(c + 2, 4), lax.rem(beside + 2, 4)]
    return [lax.rem(c + i, cuts) for i in range(cuts)]


def kernel(
    devices,
    cuts,
    cap,
    lengths,
    routes,
    route_weight,
    queries,
    keys,
    values,
    residual,
    gate,
    up,
    down,
    out,
    q_buf,
    k_buf,
    v_buf,
    res_buf,
    q_rows,
    att_rows,
    hidden,
    wg,
    wu,
    wd,
    outgoing,
    arrived,
    stacked,
    gate_act,
    up_act,
    act,
    cut_send,
    cut_recv,
    own,
    paired,
    back_send,
    back_recv,
    in_sem,
    wg_sem,
    wu_sem,
    wd_sem,
    row_send,
    row_recv,
    share_send,
    share_recv,
    sum_send,
    sum_recv,
    ret_send,
    ret_recv,
):
    b = lax.axis_index("expert")
    c = lax.axis_index("cuts")
    order = cut_order(c, cuts)
    row_count, width = q_buf.shape
    context = k_buf.shape[1]
    kv_local = k_buf.shape[2] // HEAD
    group = HEADS // KV_HEADS
    stride = kv_local * SLOTS
    splits = devices // EXPERTS
    half = width // 2
    ff = wg.shape[2]

    barrier = pltpu.get_barrier_semaphore()

    def greet(i):
        pl.semaphore_signal(
            barrier, inc=1, device_id={"expert": lax.rem(b + i, devices)}, device_id_type=MESH
        )

    each(1, devices, greet)
    for peer in order[1:]:
        pl.semaphore_signal(barrier, inc=1, device_id={"cuts": peer}, device_id_type=MESH)

    loads = [
        pltpu.make_async_copy(queries, q_buf, in_sem.at[0]),
        pltpu.make_async_copy(keys, k_buf, in_sem.at[1]),
        pltpu.make_async_copy(values, v_buf, in_sem.at[2]),
        pltpu.make_async_copy(residual, res_buf, in_sem.at[3]),
    ]
    gate_loads, up_loads, down_loads = [], [], []
    for i in range(cuts):
        rows = pl.ds(pl.multiple_of(order[i] * width, width), width)
        gate_loads.append(pltpu.make_async_copy(gate.at[0, rows, :], wg.at[i], wg_sem.at[i]))
        up_loads.append(pltpu.make_async_copy(up.at[0, rows, :], wu.at[i], wu_sem.at[i]))
    for i in range(cuts):
        columns = pl.ds(pl.multiple_of(order[cuts - 1 - i] * width, width), width)
        down_loads.append(pltpu.make_async_copy(down.at[0, :, columns], wd.at[i], wd_sem.at[i]))
    for load in loads:
        load.start()

    slot = lax.broadcasted_iota(jnp.int32, (EXPERTS * cap, row_count), 0)
    expert_of = slot // cap
    routed = jnp.zeros((EXPERTS * cap, row_count), jnp.float32)
    share = jnp.zeros((EXPERTS * cap, row_count), jnp.float32)
    for k in range(TOPK):
        named = routes[k : k + 1, :] == expert_of
        routed = routed + jnp.where(named, 1.0, 0.0)
        share = share + jnp.where(named, route_weight[k : k + 1, :], 0.0)
    before = jnp.where(
        lax.broadcasted_iota(jnp.int32, (row_count, row_count), 0)
        < lax.broadcasted_iota(jnp.int32, (row_count, row_count), 1),
        1.0,
        0.0,
    )
    earlier = jnp.dot(
        routed.astype(jnp.bfloat16), before.astype(jnp.bfloat16), preferred_element_type=jnp.float32
    )
    place = (slot - expert_of * cap).astype(jnp.float32)
    chosen = jnp.where(earlier == place, routed, 0.0)
    weighted = chosen * share

    q_rows[...] = jnp.zeros_like(q_rows)
    loads[0].wait()
    for kv in range(kv_local):
        for g in range(group):
            head = kv * group + g
            q_rows[pl.ds(kv * SLOTS + g, row_count, stride=stride), :] = q_buf[
                :, head * HEAD : (head + 1) * HEAD
            ].astype(jnp.float32)
    loads[1].wait()
    loads[2].wait()
    for g, u in zip(gate_loads, up_loads):
        g.start()
        u.start()
    key_head = lax.broadcasted_iota(jnp.int32, (stride, HEAD), 0) // SLOTS
    position = lax.broadcasted_iota(jnp.int32, (stride, context), 1)
    block = min(16, row_count)

    def attend(blk, carry):
        rows = [blk * block + i for i in range(block)]
        starts = [pl.multiple_of(r * stride, stride) for r in rows]
        scores, probs = [], []
        for r, start in zip(rows, starts):
            q = q_rows[pl.ds(start, stride), :]
            q = jnp.concatenate(
                [jnp.where(key_head == kv, q, 0.0) for kv in range(kv_local)], axis=1
            ).astype(jnp.bfloat16)
            scores.append(
                lax.dot_general(
                    q, k_buf[r], (((1,), (1,)), ((), ())), preferred_element_type=jnp.float32
                )
            )
        scores = [
            jnp.where(position < lengths[r], score / math.sqrt(HEAD), -jnp.inf)
            for r, score in zip(rows, scores)
        ]
        highest = [jnp.max(score, axis=-1, keepdims=True) for score in scores]
        scaled = [jnp.exp(score - high) for score, high in zip(scores, highest)]
        sums = [jnp.sum(value, axis=-1, keepdims=True) for value in scaled]
        probs = [(value / part).astype(jnp.bfloat16) for value, part in zip(scaled, sums)]
        atts = [
            jnp.dot(prob, v_buf[r], preferred_element_type=jnp.float32)
            for r, prob in zip(rows, probs)
        ]
        for start, att in zip(starts, atts):
            for kv in range(kv_local):
                att_rows[pl.ds(start + kv * SLOTS, SLOTS), :] = att[
                    kv * SLOTS : (kv + 1) * SLOTS, kv * HEAD : (kv + 1) * HEAD
                ]
        return carry

    lax.fori_loop(0, row_count // block, attend, 0)
    loads[3].wait()
    for kv in range(kv_local):
        for g in range(group):
            columns = slice((kv * group + g) * HEAD, (kv * group + g + 1) * HEAD)
            hidden[:, columns] = (
                res_buf[:, columns].astype(jnp.float32)
                + att_rows[pl.ds(kv * SLOTS + g, row_count, stride=stride), :]
            )

    picked = jnp.dot(
        chosen.astype(jnp.bfloat16),
        hidden[...].astype(jnp.bfloat16),
        preferred_element_type=jnp.float32,
    )
    for e in range(EXPERTS):
        rows = picked[e * cap : (e + 1) * cap]
        outgoing[e] = jnp.concatenate([rows[:, :half], rows[:, half:]], axis=0).astype(jnp.bfloat16)
    arrived[c, b] = outgoing[b // splits]

    pl.semaphore_wait(barrier, devices - 1 + cuts - 1)

    def row_copy(to):
        return pltpu.make_async_remote_copy(
            src_ref=outgoing.at[to // splits],
            dst_ref=arrived.at[c, b],
            send_sem=row_send.at[to],
            recv_sem=row_recv.at[b],
            device_id={"expert": to},
            device_id_type=MESH,
        )

    each(1, devices, lambda i: row_copy(lax.rem(b + i, devices)).start())

    def forward(a):
        for peer in order[:0:-1]:
            pltpu.make_async_remote_copy(
                src_ref=arrived.at[c, a],
                dst_ref=arrived.at[c, a],
                send_sem=share_send.at[peer],
                recv_sem=share_recv.at[c],
                device_id={"cuts": peer},
                device_id_type=MESH,
            ).start()

    forward(b)
    for d in down_loads:
        d.start()

    def take(i):
        a = lax.rem(b + devices - i, devices)
        pltpu.make_async_remote_copy(
            src_ref=arrived.at[c, a],
            dst_ref=arrived.at[c, a],
            send_sem=row_send.at[a],
            recv_sem=row_recv.at[a],
            device_id={"expert": a},
            device_id_type=MESH,
        ).wait_recv()
        forward(a)

    each(1, devices, take)

    def whole_share(peer):
        return pltpu.make_async_remote_copy(
            src_ref=arrived.at[peer],
            dst_ref=arrived.at[peer],
            send_sem=share_send.at[peer],
            recv_sem=share_recv.at[peer],
            device_id={"cuts": peer},
            device_id_type=MESH,
        )

    tile = 512 if ff % 512 == 0 else ff
    for i in range(cuts):
        if i:
            whole_share(order[i]).wait_recv()

        def pack(pair, i=i):
            first = arrived[order[i], 2 * pair].astype(jnp.float32)
            second = arrived[order[i], 2 * pair + 1].astype(jnp.float32)
            rows = pl.ds(pair * 2 * cap, 2 * cap)
            stacked[rows, :half] = jnp.concatenate([first[:cap], second[:cap]], axis=0).astype(
                jnp.bfloat16
            )
            stacked[rows, half:] = jnp.concatenate([first[cap:], second[cap:]], axis=0).astype(
                jnp.bfloat16
            )

        each(0, devices // 2, pack)
        gate_loads[i].wait()
        up_loads[i].wait()

        def project(n, carry, i=i):
            columns = pl.ds(pl.multiple_of(n * tile, tile), tile)
            x = stacked[...]
            for weight, total in ((wg, gate_act), (wu, up_act)):
                part = jnp.dot(x, weight[i, :, columns], preferred_element_type=jnp.float32)
                total[:, columns] = part if i == 0 else total[:, columns] + part
            return carry

        lax.fori_loop(0, ff // tile, project, 0)

    gated = gate_act[...]
    act[...] = (gated / (1.0 + jnp.exp(-gated)) * up_act[...]).astype(jnp.bfloat16)

    def sum_copy(j):
        peer = order[1] if cuts == 4 and j == 0 else order[cuts - 1 - j]
        return pltpu.make_async_remote_copy(
            src_ref=cut_send.at[j],
            dst_ref=cut_recv.at[order[2] if cuts == 4 and j == 0 else c],
            send_sem=sum_send.at[j],
            recv_sem=sum_recv.at[order[2] if cuts == 4 and j == 0 else c],
            device_id={"cuts": peer},
            device_id_type=MESH,
        )

    def sum_arrived(peer):
        pltpu.make_async_remote_copy(
            src_ref=cut_recv.at[peer],
            dst_ref=cut_recv.at[peer],
            send_sem=sum_send.at[0],
            recv_sem=sum_recv.at[peer],
            device_id={"cuts": peer},
            device_id_type=MESH,
        ).wait_recv()

    out_tile = half if half % 128 == 0 else width
    for j in range(cuts):
        down_loads[j].wait()

        def expand(n, carry, j=j):
            columns = pl.ds(pl.multiple_of(n * out_tile, out_tile), out_tile)
            part = jnp.dot(act[...], wd[j, :, columns], preferred_element_type=jnp.float32)
            if cuts == 4 and j == 1:
                paired[:, columns] = part
            elif j < cuts - 1:
                cut_send[j, :, columns] = part.astype(jnp.bfloat16)
            else:
                own[:, columns] = part
            return carry

        lax.fori_loop(0, width // out_tile, expand, 0)
        if cuts == 4 and j == 2:
            sum_copy(2).start()
            sum_arrived(order[3])
            items = paired.shape[0]

            def pair_sum(n):
                rows = pl.ds(n * 2 * cap, 2 * cap)
                both = paired[rows, :] + cut_recv[order[3], rows, :].astype(jnp.float32)
                cut_send[1, rows, :] = both.astype(jnp.bfloat16)

            each(0, items // (2 * cap), pair_sum)
            sum_copy(1).start()
        elif j < cuts - 1 and not (cuts == 4 and j == 1):
            sum_copy(j).start()

    senders = [order[1], order[2]] if cuts == 4 else order[1:]
    for peer in senders:
        sum_arrived(peer)

    def total(pair):
        rows = pl.ds(pair * 2 * cap, 2 * cap)
        value = own[rows, :]
        for peer in senders:
            value = value + cut_recv[peer, rows, :].astype(jnp.float32)
        for k in range(2):
            mine = value[k * cap : (k + 1) * cap]
            back_send[2 * pair + k] = jnp.concatenate(
                [mine[:, :half], mine[:, half:]], axis=0
            ).astype(jnp.bfloat16)

    each(0, devices // 2, total)

    def back_copy(to):
        return pltpu.make_async_remote_copy(
            src_ref=back_send.at[to],
            dst_ref=back_recv.at[b],
            send_sem=ret_send.at[to],
            recv_sem=ret_recv.at[b],
            device_id={"expert": to},
            device_id_type=MESH,
        )

    each(1, devices, lambda i: back_copy(lax.rem(b + i, devices)).start())
    back_recv[b] = back_send[b]

    each(1, devices, lambda i: row_copy(lax.rem(b + i, devices)).wait_send())
    for peer in order[1:]:
        whole_share(peer).wait_send()
    for j in range(cuts - 1):
        sum_copy(j).wait_send()

    def returned(i):
        a = lax.rem(b + devices - i, devices)
        pltpu.make_async_remote_copy(
            src_ref=back_recv.at[a],
            dst_ref=back_recv.at[a],
            send_sem=ret_send.at[a],
            recv_sem=ret_recv.at[a],
            device_id={"expert": a},
            device_id_type=MESH,
        ).wait_recv()

    each(1, devices, returned)
    sums = []
    for e in range(EXPERTS):
        value = back_recv[e * splits].astype(jnp.float32)
        for s in range(1, splits):
            value = value + back_recv[e * splits + s].astype(jnp.float32)
        sums.append(value)
    for h in range(2):
        columns = slice(h * half, (h + 1) * half)
        stack = jnp.concatenate([value[h * cap : (h + 1) * cap] for value in sums], axis=0)
        combined = lax.dot_general(
            weighted,
            stack,
            (((0,), (0,)), ((), ())),
            preferred_element_type=jnp.float32,
            precision=lax.Precision.HIGHEST,
        )
        out[:, columns] = (hidden[:, columns] + combined).astype(jnp.bfloat16)
    each(1, devices, lambda i: back_copy(lax.rem(b + i, devices)).wait_send())


def on_device(
    devices,
    cuts,
    queries,
    key_cache,
    value_cache,
    lengths,
    residual,
    routes,
    route_weight,
    gate_weight,
    up_weight,
    down_weight,
):
    row_count, width = queries.shape
    cap = (row_count * TOPK + MODEL_EXPERTS - 1) // MODEL_EXPERTS
    ff = gate_weight.shape[2]
    kv_width = key_cache.shape[2]
    stride = kv_width // HEAD * SLOTS
    items = devices * cap
    bf16, f32 = jnp.bfloat16, jnp.float32
    dma = pltpu.SemaphoreType.DMA
    vmem = pl.BlockSpec(memory_space=pltpu.VMEM)
    anywhere = pl.BlockSpec(memory_space=pl.ANY)
    return pl.pallas_call(
        functools.partial(kernel, devices, cuts, cap),
        out_shape=jax.ShapeDtypeStruct((row_count, width), bf16),
        in_specs=[pl.BlockSpec(memory_space=pltpu.SMEM), vmem, vmem] + [anywhere] * 7,
        out_specs=vmem,
        scratch_shapes=[
            pltpu.VMEM((row_count, width), bf16),
            pltpu.VMEM(key_cache.shape, bf16),
            pltpu.VMEM(value_cache.shape, bf16),
            pltpu.VMEM((row_count, width), bf16),
            pltpu.VMEM((row_count * stride, HEAD), f32),
            pltpu.VMEM((row_count * stride, HEAD), f32),
            pltpu.VMEM((row_count, width), f32),
            pltpu.VMEM((cuts, width, ff), bf16),
            pltpu.VMEM((cuts, width, ff), bf16),
            pltpu.VMEM((cuts, ff, width), bf16),
            pltpu.VMEM((EXPERTS, 2 * cap, width // 2), bf16),
            pltpu.VMEM((cuts, devices, 2 * cap, width // 2), bf16),
            pltpu.VMEM((items, width), bf16),
            pltpu.VMEM((items, ff), f32),
            pltpu.VMEM((items, ff), f32),
            pltpu.VMEM((items, ff), bf16),
            pltpu.VMEM((cuts - 1, items, width), bf16),
            pltpu.VMEM((cuts, items, width), bf16),
            pltpu.VMEM((items, width), f32),
            pltpu.VMEM((items, width), f32),
            pltpu.VMEM((devices, 2 * cap, width // 2), bf16),
            pltpu.VMEM((devices, 2 * cap, width // 2), bf16),
            dma((4,)),
            dma((cuts,)),
            dma((cuts,)),
            dma((cuts,)),
            dma((devices,)),
            dma((devices,)),
            dma((cuts,)),
            dma((cuts,)),
            dma((cuts - 1,)),
            dma((cuts,)),
            dma((devices,)),
            dma((devices,)),
        ],
        compiler_params=pltpu.CompilerParams(
            collective_id=0, has_side_effects=True, vmem_limit_bytes=60 * 1024 * 1024
        ),
    )(
        lengths,
        routes.T,
        route_weight.T,
        queries,
        key_cache,
        value_cache,
        residual,
        gate_weight,
        up_weight,
        down_weight,
    )


def solution(mesh):
    return jax.shard_map(
        functools.partial(on_device, mesh.shape["expert"], mesh.shape["cuts"]),
        mesh=mesh,
        in_specs=(
            P(("groups", "expert"), "cuts"),
            P(("groups", "expert"), None, "cuts"),
            P(("groups", "expert"), None, "cuts"),
            P(("groups", "expert")),
            P(("groups", "expert"), "cuts"),
            P(("groups", "expert"), None),
            P(("groups", "expert"), None),
            P("expert", None, "cuts"),
            P("expert", None, "cuts"),
            P("expert", "cuts", None),
        ),
        out_specs=P(("groups", "expert"), "cuts"),
        check_vma=False,
    )
```

```python
import functools
import math

import jax
import jax.numpy as jnp
from jax import lax
from jax.experimental import pallas as pl
from jax.experimental.pallas import tpu as pltpu
from jax.sharding import PartitionSpec as P

HEADS = 48
KV_HEADS = 8
HEAD = 128
MODEL_EXPERTS = 16
TOPK = 4
EXPERTS = 2
SLOTS = 8
MESH = pl.DeviceIdType.MESH


def each(low, high, body):
    if high - low <= 8:
        for i in range(low, high):
            body(i)
    else:

        def step(i, carry):
            body(i)
            return carry

        lax.fori_loop(low, high, step, 0)


def cut_order(c, cuts):
    if cuts == 4:
        beside = c + 1 - 2 * lax.rem(c, 2)
        return [c, beside, lax.rem(c + 2, 4), lax.rem(beside + 2, 4)]
    return [lax.rem(c + i, cuts) for i in range(cuts)]


def kernel(
    devices,
    cuts,
    cap,
    lengths,
    routes,
    route_weight,
    queries,
    keys,
    values,
    residual,
    gate,
    up,
    down,
    out,
    q_buf,
    k_buf,
    v_buf,
    res_buf,
    q_rows,
    att_rows,
    hidden,
    wg,
    wu,
    wd,
    outgoing,
    arrived,
    stacked,
    gate_act,
    up_act,
    act,
    cut_send,
    cut_recv,
    own,
    paired,
    back_send,
    back_recv,
    in_sem,
    wg_sem,
    wu_sem,
    wd_sem,
    row_send,
    row_recv,
    share_send,
    share_recv,
    sum_send,
    sum_recv,
    ret_send,
    ret_recv,
):
    b = lax.axis_index("expert")
    c = lax.axis_index("cuts")
    order = cut_order(c, cuts)
    row_count, width = q_buf.shape
    context = k_buf.shape[1]
    kv_local = k_buf.shape[2] // HEAD
    group = HEADS // KV_HEADS
    stride = kv_local * SLOTS
    splits = devices // EXPERTS
    half = width // 2
    ff = wg.shape[2]

    barrier = pltpu.get_barrier_semaphore()

    def greet(i):
        pl.semaphore_signal(
            barrier, inc=1, device_id={"expert": lax.rem(b + i, devices)}, device_id_type=MESH
        )

    each(1, devices, greet)
    for peer in order[1:]:
        pl.semaphore_signal(barrier, inc=1, device_id={"cuts": peer}, device_id_type=MESH)

    loads = [
        pltpu.make_async_copy(queries, q_buf, in_sem.at[0]),
        pltpu.make_async_copy(keys, k_buf, in_sem.at[1]),
        pltpu.make_async_copy(values, v_buf, in_sem.at[2]),
        pltpu.make_async_copy(residual, res_buf, in_sem.at[3]),
    ]
    gate_loads, up_loads, down_loads = [], [], []
    for i in range(cuts):
        rows = pl.ds(pl.multiple_of(order[i] * width, width), width)
        gate_loads.append(pltpu.make_async_copy(gate.at[0, rows, :], wg.at[i], wg_sem.at[i]))
        up_loads.append(pltpu.make_async_copy(up.at[0, rows, :], wu.at[i], wu_sem.at[i]))
    for i in range(cuts):
        columns = pl.ds(pl.multiple_of(order[cuts - 1 - i] * width, width), width)
        down_loads.append(pltpu.make_async_copy(down.at[0, :, columns], wd.at[i], wd_sem.at[i]))
    for load in loads:
        load.start()

    slot = lax.broadcasted_iota(jnp.int32, (EXPERTS * cap, row_count), 0)
    expert_of = slot // cap
    routed = jnp.zeros((EXPERTS * cap, row_count), jnp.float32)
    share = jnp.zeros((EXPERTS * cap, row_count), jnp.float32)
    for k in range(TOPK):
        named = routes[k : k + 1, :] == expert_of
        routed = routed + jnp.where(named, 1.0, 0.0)
        share = share + jnp.where(named, route_weight[k : k + 1, :], 0.0)
    before = jnp.where(
        lax.broadcasted_iota(jnp.int32, (row_count, row_count), 0)
        < lax.broadcasted_iota(jnp.int32, (row_count, row_count), 1),
        1.0,
        0.0,
    )
    earlier = jnp.dot(
        routed.astype(jnp.bfloat16), before.astype(jnp.bfloat16), preferred_element_type=jnp.float32
    )
    place = (slot - expert_of * cap).astype(jnp.float32)
    chosen = jnp.where(earlier == place, routed, 0.0)
    weighted = chosen * share

    q_rows[...] = jnp.zeros_like(q_rows)
    loads[0].wait()
    for kv in range(kv_local):
        for g in range(group):
            head = kv * group + g
            q_rows[pl.ds(kv * SLOTS + g, row_count, stride=stride), :] = q_buf[
                :, head * HEAD : (head + 1) * HEAD
            ].astype(jnp.float32)
    loads[1].wait()
    loads[2].wait()
    for g, u in zip(gate_loads, up_loads):
        g.start()
        u.start()
    key_head = lax.broadcasted_iota(jnp.int32, (stride, HEAD), 0) // SLOTS
    position = lax.broadcasted_iota(jnp.int32, (stride, context), 1)
    block = min(16, row_count)

    def attend(blk, carry):
        rows = [blk * block + i for i in range(block)]
        starts = [pl.multiple_of(r * stride, stride) for r in rows]
        scores, probs = [], []
        for r, start in zip(rows, starts):
            q = q_rows[pl.ds(start, stride), :]
            q = jnp.concatenate(
                [jnp.where(key_head == kv, q, 0.0) for kv in range(kv_local)], axis=1
            ).astype(jnp.bfloat16)
            scores.append(
                lax.dot_general(
                    q, k_buf[r], (((1,), (1,)), ((), ())), preferred_element_type=jnp.float32
                )
            )
        scores = [
            jnp.where(position < lengths[r], score / math.sqrt(HEAD), -jnp.inf)
            for r, score in zip(rows, scores)
        ]
        highest = [jnp.max(score, axis=-1, keepdims=True) for score in scores]
        scaled = [jnp.exp(score - high) for score, high in zip(scores, highest)]
        sums = [jnp.sum(value, axis=-1, keepdims=True) for value in scaled]
        probs = [(value / part).astype(jnp.bfloat16) for value, part in zip(scaled, sums)]
        atts = [
            jnp.dot(prob, v_buf[r], preferred_element_type=jnp.float32)
            for r, prob in zip(rows, probs)
        ]
        for start, att in zip(starts, atts):
            for kv in range(kv_local):
                att_rows[pl.ds(start + kv * SLOTS, SLOTS), :] = att[
                    kv * SLOTS : (kv + 1) * SLOTS, kv * HEAD : (kv + 1) * HEAD
                ]
        return carry

    lax.fori_loop(0, row_count // block, attend, 0)
    loads[3].wait()
    for kv in range(kv_local):
        for g in range(group):
            columns = slice((kv * group + g) * HEAD, (kv * group + g + 1) * HEAD)
            hidden[:, columns] = (
                res_buf[:, columns].astype(jnp.float32)
                + att_rows[pl.ds(kv * SLOTS + g, row_count, stride=stride), :]
            )

    picked = jnp.dot(
        chosen.astype(jnp.bfloat16),
        hidden[...].astype(jnp.bfloat16),
        preferred_element_type=jnp.float32,
    )
    for e in range(EXPERTS):
        rows = picked[e * cap : (e + 1) * cap]
        outgoing[e] = jnp.concatenate([rows[:, :half], rows[:, half:]], axis=0).astype(jnp.bfloat16)
    arrived[c, b] = outgoing[b // splits]

    pl.semaphore_wait(barrier, devices - 1 + cuts - 1)

    def row_copy(to):
        return pltpu.make_async_remote_copy(
            src_ref=outgoing.at[to // splits],
            dst_ref=arrived.at[c, b],
            send_sem=row_send.at[to],
            recv_sem=row_recv.at[b],
            device_id={"expert": to},
            device_id_type=MESH,
        )

    each(1, devices, lambda i: row_copy(lax.rem(b + i, devices)).start())

    nearest = [order[2], order[1]] if cuts == 4 else order[1:]

    def forward(a):
        for peer in nearest:
            pltpu.make_async_remote_copy(
                src_ref=arrived.at[c, a],
                dst_ref=arrived.at[c, a],
                send_sem=share_send.at[peer],
                recv_sem=share_recv.at[c],
                device_id={"cuts": peer},
                device_id_type=MESH,
            ).start()

    forward(b)
    for d in down_loads:
        d.start()

    def take(i):
        a = lax.rem(b + devices - i, devices)
        pltpu.make_async_remote_copy(
            src_ref=arrived.at[c, a],
            dst_ref=arrived.at[c, a],
            send_sem=row_send.at[a],
            recv_sem=row_recv.at[a],
            device_id={"expert": a},
            device_id_type=MESH,
        ).wait_recv()
        forward(a)

    each(1, devices, take)

    def whole_share(peer):
        return pltpu.make_async_remote_copy(
            src_ref=arrived.at[peer],
            dst_ref=arrived.at[peer],
            send_sem=share_send.at[peer],
            recv_sem=share_recv.at[peer],
            device_id={"cuts": peer},
            device_id_type=MESH,
        )

    def relay():
        return pltpu.make_async_remote_copy(
            src_ref=arrived.at[order[2]],
            dst_ref=arrived.at[order[2]],
            send_sem=share_send.at[c],
            recv_sem=share_recv.at[order[2]],
            device_id={"cuts": order[1]},
            device_id_type=MESH,
        )

    tile = 512 if ff % 512 == 0 else ff
    for i in range(cuts):
        if cuts == 4 and i == 1:
            whole_share(order[2]).wait_recv()
            relay().start()
        if i and not (cuts == 4 and i == 2):
            whole_share(order[i]).wait_recv()

        def pack(pair, i=i):
            first = arrived[order[i], 2 * pair].astype(jnp.float32)
            second = arrived[order[i], 2 * pair + 1].astype(jnp.float32)
            rows = pl.ds(pair * 2 * cap, 2 * cap)
            stacked[rows, :half] = jnp.concatenate([first[:cap], second[:cap]], axis=0).astype(
                jnp.bfloat16
            )
            stacked[rows, half:] = jnp.concatenate([first[cap:], second[cap:]], axis=0).astype(
                jnp.bfloat16
            )

        each(0, devices // 2, pack)
        gate_loads[i].wait()
        up_loads[i].wait()

        def project(n, carry, i=i):
            columns = pl.ds(pl.multiple_of(n * tile, tile), tile)
            x = stacked[...]
            for weight, total in ((wg, gate_act), (wu, up_act)):
                part = jnp.dot(x, weight[i, :, columns], preferred_element_type=jnp.float32)
                total[:, columns] = part if i == 0 else total[:, columns] + part
            return carry

        lax.fori_loop(0, ff // tile, project, 0)

    gated = gate_act[...]
    act[...] = (gated / (1.0 + jnp.exp(-gated)) * up_act[...]).astype(jnp.bfloat16)

    def sum_copy(j):
        peer = order[1] if cuts == 4 and j == 0 else order[cuts - 1 - j]
        return pltpu.make_async_remote_copy(
            src_ref=cut_send.at[j],
            dst_ref=cut_recv.at[order[2] if cuts == 4 and j == 0 else c],
            send_sem=sum_send.at[j],
            recv_sem=sum_recv.at[order[2] if cuts == 4 and j == 0 else c],
            device_id={"cuts": peer},
            device_id_type=MESH,
        )

    def sum_arrived(peer):
        pltpu.make_async_remote_copy(
            src_ref=cut_recv.at[peer],
            dst_ref=cut_recv.at[peer],
            send_sem=sum_send.at[0],
            recv_sem=sum_recv.at[peer],
            device_id={"cuts": peer},
            device_id_type=MESH,
        ).wait_recv()

    out_tile = half if half % 128 == 0 else width
    for j in range(cuts):
        down_loads[j].wait()

        def expand(n, carry, j=j):
            columns = pl.ds(pl.multiple_of(n * out_tile, out_tile), out_tile)
            part = jnp.dot(act[...], wd[j, :, columns], preferred_element_type=jnp.float32)
            if cuts == 4 and j == 1:
                paired[:, columns] = part
            elif j < cuts - 1:
                cut_send[j, :, columns] = part.astype(jnp.bfloat16)
            else:
                own[:, columns] = part
            return carry

        lax.fori_loop(0, width // out_tile, expand, 0)
        if cuts == 4 and j == 2:
            sum_copy(2).start()
            sum_arrived(order[3])
            items = paired.shape[0]

            def pair_sum(n):
                rows = pl.ds(n * 2 * cap, 2 * cap)
                both = paired[rows, :] + cut_recv[order[3], rows, :].astype(jnp.float32)
                cut_send[1, rows, :] = both.astype(jnp.bfloat16)

            each(0, items // (2 * cap), pair_sum)
            sum_copy(1).start()
        elif j < cuts - 1 and not (cuts == 4 and j == 1):
            sum_copy(j).start()

    senders = [order[1], order[2]] if cuts == 4 else order[1:]
    for peer in senders:
        sum_arrived(peer)

    def total(pair):
        rows = pl.ds(pair * 2 * cap, 2 * cap)
        value = own[rows, :]
        for peer in senders:
            value = value + cut_recv[peer, rows, :].astype(jnp.float32)
        for k in range(2):
            mine = value[k * cap : (k + 1) * cap]
            back_send[2 * pair + k] = jnp.concatenate(
                [mine[:, :half], mine[:, half:]], axis=0
            ).astype(jnp.bfloat16)

    each(0, devices // 2, total)

    def back_copy(to):
        return pltpu.make_async_remote_copy(
            src_ref=back_send.at[to],
            dst_ref=back_recv.at[b],
            send_sem=ret_send.at[to],
            recv_sem=ret_recv.at[b],
            device_id={"expert": to},
            device_id_type=MESH,
        )

    each(1, devices, lambda i: back_copy(lax.rem(b + i, devices)).start())
    back_recv[b] = back_send[b]

    each(1, devices, lambda i: row_copy(lax.rem(b + i, devices)).wait_send())
    for peer in nearest:
        whole_share(peer).wait_send()
    if cuts == 4:
        relay().wait_send()
    for j in range(cuts - 1):
        sum_copy(j).wait_send()

    def returned(i):
        a = lax.rem(b + devices - i, devices)
        pltpu.make_async_remote_copy(
            src_ref=back_recv.at[a],
            dst_ref=back_recv.at[a],
            send_sem=ret_send.at[a],
            recv_sem=ret_recv.at[a],
            device_id={"expert": a},
            device_id_type=MESH,
        ).wait_recv()

    each(1, devices, returned)
    sums = []
    for e in range(EXPERTS):
        value = back_recv[e * splits].astype(jnp.float32)
        for s in range(1, splits):
            value = value + back_recv[e * splits + s].astype(jnp.float32)
        sums.append(value)
    for h in range(2):
        columns = slice(h * half, (h + 1) * half)
        stack = jnp.concatenate([value[h * cap : (h + 1) * cap] for value in sums], axis=0)
        combined = lax.dot_general(
            weighted,
            stack,
            (((0,), (0,)), ((), ())),
            preferred_element_type=jnp.float32,
            precision=lax.Precision.HIGHEST,
        )
        out[:, columns] = (hidden[:, columns] + combined).astype(jnp.bfloat16)
    each(1, devices, lambda i: back_copy(lax.rem(b + i, devices)).wait_send())


def on_device(
    devices,
    cuts,
    queries,
    key_cache,
    value_cache,
    lengths,
    residual,
    routes,
    route_weight,
    gate_weight,
    up_weight,
    down_weight,
):
    row_count, width = queries.shape
    cap = (row_count * TOPK + MODEL_EXPERTS - 1) // MODEL_EXPERTS
    ff = gate_weight.shape[2]
    kv_width = key_cache.shape[2]
    stride = kv_width // HEAD * SLOTS
    items = devices * cap
    bf16, f32 = jnp.bfloat16, jnp.float32
    dma = pltpu.SemaphoreType.DMA
    vmem = pl.BlockSpec(memory_space=pltpu.VMEM)
    anywhere = pl.BlockSpec(memory_space=pl.ANY)
    return pl.pallas_call(
        functools.partial(kernel, devices, cuts, cap),
        out_shape=jax.ShapeDtypeStruct((row_count, width), bf16),
        in_specs=[pl.BlockSpec(memory_space=pltpu.SMEM), vmem, vmem] + [anywhere] * 7,
        out_specs=vmem,
        scratch_shapes=[
            pltpu.VMEM((row_count, width), bf16),
            pltpu.VMEM(key_cache.shape, bf16),
            pltpu.VMEM(value_cache.shape, bf16),
            pltpu.VMEM((row_count, width), bf16),
            pltpu.VMEM((row_count * stride, HEAD), f32),
            pltpu.VMEM((row_count * stride, HEAD), f32),
            pltpu.VMEM((row_count, width), f32),
            pltpu.VMEM((cuts, width, ff), bf16),
            pltpu.VMEM((cuts, width, ff), bf16),
            pltpu.VMEM((cuts, ff, width), bf16),
            pltpu.VMEM((EXPERTS, 2 * cap, width // 2), bf16),
            pltpu.VMEM((cuts, devices, 2 * cap, width // 2), bf16),
            pltpu.VMEM((items, width), bf16),
            pltpu.VMEM((items, ff), f32),
            pltpu.VMEM((items, ff), f32),
            pltpu.VMEM((items, ff), bf16),
            pltpu.VMEM((cuts - 1, items, width), bf16),
            pltpu.VMEM((cuts, items, width), bf16),
            pltpu.VMEM((items, width), f32),
            pltpu.VMEM((items, width), f32),
            pltpu.VMEM((devices, 2 * cap, width // 2), bf16),
            pltpu.VMEM((devices, 2 * cap, width // 2), bf16),
            dma((4,)),
            dma((cuts,)),
            dma((cuts,)),
            dma((cuts,)),
            dma((devices,)),
            dma((devices,)),
            dma((cuts,)),
            dma((cuts,)),
            dma((cuts - 1,)),
            dma((cuts,)),
            dma((devices,)),
            dma((devices,)),
        ],
        compiler_params=pltpu.CompilerParams(
            collective_id=0, has_side_effects=True, vmem_limit_bytes=60 * 1024 * 1024
        ),
    )(
        lengths,
        routes.T,
        route_weight.T,
        queries,
        key_cache,
        value_cache,
        residual,
        gate_weight,
        up_weight,
        down_weight,
    )


def solution(mesh):
    return jax.shard_map(
        functools.partial(on_device, mesh.shape["expert"], mesh.shape["cuts"]),
        mesh=mesh,
        in_specs=(
            P(("groups", "expert"), "cuts"),
            P(("groups", "expert"), None, "cuts"),
            P(("groups", "expert"), None, "cuts"),
            P(("groups", "expert")),
            P(("groups", "expert"), "cuts"),
            P(("groups", "expert"), None),
            P(("groups", "expert"), None),
            P("expert", None, "cuts"),
            P("expert", None, "cuts"),
            P("expert", "cuts", None),
        ),
        out_specs=P(("groups", "expert"), "cuts"),
        check_vma=False,
    )
```
